256 devices in a mesh: clip: 16 (over x, z_hi, core), seq: 16 (over y, z_lo).
Axes of the slice: x: 4, y: 4, z: 8 (z_hi: 2, z_lo: 4; z = z_hi * 4 + z_lo), core: 2. Of those that a mesh axis runs over, the one named last changes fastest.
Arguments:
- video_query: bfloat16 [32768, 4096], P(('clip', 'seq')), parts along dimension 0
- video_key: bfloat16 [32768, 4096], P(('clip', 'seq')), parts along dimension 0
- video_value: bfloat16 [32768, 4096], P(('clip', 'seq')), parts along dimension 0, may hold values from -6 to 6
- cross_query: bfloat16 [32768, 4096], P(('clip', 'seq')), parts along dimension 0
- text_rows: bfloat16 [8192, 4096], P(('clip', 'seq')), parts along dimension 0, may hold values from -6 to 6
- text_block: int32 [256], P('clip'), parts along dimension 0, may hold values from 0 to 15, each once
- text_length: int32 [16], P('clip'), parts along dimension 0, may hold values from 64 to 512
- key_weight: bfloat16 [4096, 4096], P(None, 'seq'), may hold values from -0.09375 to 0.09375
- value_weight: bfloat16 [4096, 4096], P(None, 'seq'), may hold values from -0.09375 to 0.09375
Outputs:
- self_out: bfloat16 [32768, 4096], P(('clip', 'seq')), parts along dimension 0
- cross_out: bfloat16 [32768, 4096], P(('clip', 'seq')), parts along dimension 0
The draws below stay inside these ranges and needn't reach their ends.
There are 16 independent parts, one for each index of `clip`. The reference program is written for one: setup_inputs(seed, part) draws one part's arguments, and reference() takes and returns one part's arrays. A program takes and returns all parts, laid end to end along the dimension named above; an argument that names none is the same for every part. Nothing has to cross between parts.
Inputs may be any that keep to these rules, and one draw needn't show every extreme that they name: A permutation: arrival block j holds prompt rows text_block[j] * 32 onward.
All inputs are finite; a program needn't handle non-finite values.
Results may differ from the reference program's by a relative error of at most 0.012.
The reference program's roundings to bfloat16 on the way count: a program that leaves them out, or rounds other values in their place, can miss the bound.
Values may be sent and summed in bfloat16 or wider, within the bound.
No kernel may reach another device: no remote copies, remote signals or barrier semaphores. Data moves between devices by JAX's collectives and lax.ppermute only.
A program may use at most 128 MiB of HBM per device.

```python
import jax
import jax.numpy as jnp
from jax import lax

D_TEXT = 4096
HEAD_DIM = 128
TEXT = 512
INNER = 4096
TOKENS = 2048
TXT_DEV = 32
N_SEQ = 16


def drawn_pair(key):
    key_seed = jax.random.fold_in(key, 11)
    query_seed = jax.random.fold_in(key, 12)
    key_rows = jnp.clip(jax.random.normal(key_seed, (TOKENS, INNER), jnp.float32), -6.0, 6.0)
    base = jnp.clip(jax.random.normal(query_seed, (TOKENS, INNER), jnp.float32), -6.0, 6.0) * 2.5
    queries = base
    return (queries, key_rows)


def draw_video_query(key, part):
    queries, key_rows = drawn_pair(key)
    return queries.astype(jnp.bfloat16)


def draw_video_key(key, part):
    queries, key_rows = drawn_pair(key)
    return key_rows.astype(jnp.bfloat16)


def draw_cross_query(key, part):
    base_seed = jax.random.fold_in(key, 21)
    base = jnp.clip(jax.random.normal(base_seed, (TOKENS, INNER), jnp.float32), -6.0, 6.0) * 2.5
    return base.astype(jnp.bfloat16)


def draw_text_length(key, part):
    drawn = jax.random.randint(jax.random.fold_in(key, 31), (1,), TEXT // 8, TEXT + 1)
    coin = jax.random.randint(jax.random.fold_in(key, 32), (1,), 0, 4)
    full_value = jnp.full((1,), TEXT, dtype=jnp.int32)
    return jnp.where(coin == 0, full_value, drawn).astype(jnp.int32)


def block_scale(stream_key, extent, cuts, low, largest):
    def one(axis_at, shards_of):
        heights = jax.random.uniform(jax.random.fold_in(jax.random.fold_in(stream_key, 6), axis_at), (shards_of,), jnp.float32, low / len(cuts), largest / len(cuts))
        return jnp.repeat(jnp.exp(heights), extent[axis_at] // shards_of).reshape((-1,) + (1,) * (len(extent) - axis_at - 1))

    loudness = one(*cuts[0])
    for cut in cuts[1:]:
        loudness = loudness * one(*cut)
    return loudness


def normal_values(key, extent, spread, bound, split=(), kind=jnp.bfloat16):
    entries = spread * jax.random.normal(key, extent, jnp.float32)
    if split:
        entries = entries * block_scale(key, extent, split, -0.22, 0.18)
    return jnp.clip(entries, -bound, bound).astype(kind)


def setup_inputs(seed: int = 0, part: int = 0) -> dict:
    splits = jax.random.split(jax.random.key(seed), 10)
    part_keys = jax.random.split(jax.random.fold_in(splits[9], part), 10)
    return {
        "video_query": draw_video_query(jax.random.fold_in(jax.random.fold_in(splits[9], part), 71), part),
        "video_key": draw_video_key(jax.random.fold_in(jax.random.fold_in(splits[9], part), 71), part),
        "video_value": normal_values(part_keys[2], (TOKENS, INNER), 1.0, 6.0, ((0, 16),)),
        "cross_query": draw_cross_query(jax.random.fold_in(jax.random.fold_in(splits[9], part), 71), part),
        "text_rows": normal_values(part_keys[4], (TEXT, D_TEXT), 1.0, 6.0, ((0, 16),)),
        "text_block": jax.random.permutation(part_keys[5], N_SEQ).astype(jnp.int32),
        "text_length": draw_text_length(jax.random.fold_in(jax.random.fold_in(splits[9], part), 71), part),
        "key_weight": normal_values(splits[7], (D_TEXT, INNER), D_TEXT ** -0.5, 0.09375, ((1, 16),)),
        "value_weight": normal_values(splits[8], (D_TEXT, INNER), D_TEXT ** -0.5, 0.09375, ((1, 16),)),
    }


def attend(queries, key_rows, value_rows, key_valid):
    query_count = queries.shape[0]
    key_count = key_rows.shape[0]
    head_count = queries.shape[1] // HEAD_DIM
    score_scale = HEAD_DIM ** -0.5
    query_heads = queries.reshape(query_count, head_count, HEAD_DIM).transpose(1, 0, 2)
    key_heads = key_rows.reshape(key_count, head_count, HEAD_DIM).transpose(1, 0, 2)
    value_heads = value_rows.reshape(key_count, head_count, HEAD_DIM).transpose(1, 0, 2)

    def one_head(operands):
        head_query, head_key, head_value = operands
        scores = jnp.dot(head_query, head_key.T, preferred_element_type=jnp.float32) * score_scale
        if key_valid is not None:
            scores = jnp.where(key_valid[None, :], scores, -jnp.inf)
        highest = jnp.max(scores, axis=-1, keepdims=True)
        exponent = jnp.exp(scores - highest)
        weights = (exponent / jnp.sum(exponent, axis=-1, keepdims=True)).astype(jnp.bfloat16)
        return jnp.dot(weights, head_value, preferred_element_type=jnp.float32).astype(jnp.bfloat16)

    outputs = lax.map(one_head, (query_heads, key_heads, value_heads))
    return outputs.transpose(1, 0, 2).reshape(query_count, head_count * HEAD_DIM)


def reference(video_query, video_key, video_value, cross_query, text_rows, text_block, text_length, key_weight, value_weight):
    text_keys = jnp.dot(text_rows, key_weight, preferred_element_type=jnp.float32).astype(jnp.bfloat16)
    text_values = jnp.dot(text_rows, value_weight, preferred_element_type=jnp.float32).astype(jnp.bfloat16)
    arrival = jnp.arange(TEXT, dtype=jnp.int32)
    owners = arrival // TXT_DEV
    blocks_held = text_block[owners].astype(jnp.int32)
    key_valid = blocks_held * TXT_DEV + arrival % TXT_DEV < text_length[0]
    self_out = attend(video_query, video_key, video_value, None)
    cross_out = attend(cross_query, text_keys, text_values, key_valid)
    return self_out, cross_out
```

```python
import functools
import math

import jax
import jax.numpy as jnp
from jax import lax
from jax.experimental import pallas as pl
from jax.experimental.pallas import tpu as pltpu
from jax.sharding import PartitionSpec as P

HEAD_DIM = 128
EXP2_SCALE = HEAD_DIM**-0.5 * math.log2(math.e)


def attend_kernel(*refs, heads, sub_blocks, masked):
    if masked:
        query_ref, key_ref, value_ref, bias_ref, out_ref, wide_ref = refs
    else:
        query_ref, key_ref, value_ref, out_ref, wide_ref = refs
    width = query_ref.shape[-1]
    key_count = math.prod(key_ref.shape[:-1])

    @pl.when(pl.program_id(0) == 0)
    def _():
        values = value_ref[...].reshape(key_count, width)
        for head in range(heads):
            wide_ref[head, :, :HEAD_DIM] = values[:, head * HEAD_DIM : (head + 1) * HEAD_DIM]
            wide_ref[head, :, HEAD_DIM:] = jnp.ones((key_count, HEAD_DIM), jnp.bfloat16)

    queries = query_ref[...].reshape(-1, width)
    keys = key_ref[...].reshape(key_count, width)
    rows = queries.shape[0] // sub_blocks
    for block in range(sub_blocks):
        for head in range(heads):
            columns = slice(head * HEAD_DIM, (head + 1) * HEAD_DIM)
            scores = lax.dot_general(
                queries[block * rows : (block + 1) * rows, columns],
                keys[:, columns],
                (((1,), (1,)), ((), ())),
                preferred_element_type=jnp.float32,
            )
            if masked:
                scores = scores + bias_ref[...]
            highest = jnp.max(scores, axis=1, keepdims=True)
            weights = jnp.exp2((scores - highest) * EXP2_SCALE).astype(jnp.bfloat16)
            both = jnp.dot(weights, wide_ref[head], preferred_element_type=jnp.float32)
            result = (both[:, :HEAD_DIM] / both[:, HEAD_DIM:]).astype(jnp.bfloat16)
            per = out_ref.shape[1]
            for piece in range(rows // per):
                out_ref[block * (rows // per) + piece, :, columns] = result[
                    piece * per : (piece + 1) * per
                ]


def attend(arrays, specs, bias, shape, key_count, block_pieces, sub_blocks):
    pieces, per, width = shape
    heads = width // HEAD_DIM
    in_specs = list(specs)
    operands = list(arrays)
    if bias is not None:
        operands.append(bias)
        in_specs.append(pl.BlockSpec(bias.shape, lambda i: (0, 0)))
    queries = pieces * per
    return pl.pallas_call(
        functools.partial(
            attend_kernel, heads=heads, sub_blocks=sub_blocks, masked=bias is not None
        ),
        grid=(pieces // block_pieces,),
        in_specs=in_specs,
        out_specs=pl.BlockSpec((block_pieces, per, width), lambda i: (i, 0, 0)),
        out_shape=jax.ShapeDtypeStruct(shape, jnp.bfloat16),
        scratch_shapes=[pltpu.VMEM((heads, key_count, 2 * HEAD_DIM), jnp.bfloat16)],
        compiler_params=pltpu.CompilerParams(vmem_limit_bytes=48 * 1024 * 1024),
        cost_estimate=pl.CostEstimate(
            flops=4 * queries * key_count * width,
            bytes_accessed=2 * width * 2 * (queries + key_count),
            transcendentals=queries * key_count * heads,
        ),
    )(*operands)


def body(
    video_query,
    video_key,
    video_value,
    cross_query,
    text_rows,
    text_block,
    text_length,
    key_weight,
    value_weight,
):
    group_size = lax.axis_size("seq")
    tokens, inner = video_query.shape
    width = inner // group_size
    text_shard = text_rows.shape[0]
    total_text = group_size * text_shard

    piece = lax.all_gather(text_rows, "seq", axis=0, tiled=True)
    stacked = jnp.stack(
        [
            a.reshape(tokens, group_size, width).transpose(1, 0, 2)
            for a in (video_query, video_key, video_value, cross_query)
        ],
        axis=1,
    )
    by_head = lax.all_to_all(stacked, "seq", split_axis=0, concat_axis=0, tiled=True)

    block_pieces = 8
    self_heads = attend(
        (by_head, by_head, by_head),
        (
            pl.BlockSpec((block_pieces, None, tokens, width), lambda i: (i, 0, 0, 0)),
            pl.BlockSpec((group_size, None, tokens, width), lambda i: (0, 1, 0, 0)),
            pl.BlockSpec((group_size, None, tokens, width), lambda i: (0, 2, 0, 0)),
        ),
        None,
        (group_size, tokens, width),
        group_size * tokens,
        block_pieces,
        4,
    )
    self_out = lax.all_to_all(self_heads, "seq", split_axis=0, concat_axis=0, tiled=True)

    text_keys = jnp.dot(piece, key_weight, preferred_element_type=jnp.float32).astype(jnp.bfloat16)
    text_values = jnp.dot(piece, value_weight, preferred_element_type=jnp.float32).astype(
        jnp.bfloat16
    )
    position = (
        text_block[:, None] * text_shard + jnp.arange(text_shard, dtype=jnp.int32)[None, :]
    ).reshape(1, total_text)
    bias = jnp.where(position < text_length[0], 0.0, -jnp.inf).astype(jnp.float32)
    cross_heads = attend(
        (by_head, text_keys, text_values),
        (
            pl.BlockSpec((block_pieces, None, tokens, width), lambda i: (i, 3, 0, 0)),
            pl.BlockSpec((total_text, width), lambda i: (0, 0)),
            pl.BlockSpec((total_text, width), lambda i: (0, 0)),
        ),
        bias,
        (group_size, tokens, width),
        total_text,
        block_pieces,
        4,
    )
    cross_out = lax.all_to_all(cross_heads, "seq", split_axis=0, concat_axis=0, tiled=True)
    return tuple(
        a.transpose(1, 0, 2).reshape(tokens, inner) for a in (self_out, cross_out)
    )


def solution(mesh):
    rows = P(("clip", "seq"), None)
    return jax.shard_map(
        body,
        mesh=mesh,
        in_specs=(
            rows,
            rows,
            rows,
            rows,
            rows,
            P("clip"),
            P("clip"),
            P(None, "seq"),
            P(None, "seq"),
        ),
        out_specs=(rows, rows),
        check_vma=False,
    )
```

```python
import functools
import math

import jax
import jax.numpy as jnp
from jax import lax
from jax.experimental import pallas as pl
from jax.experimental.pallas import tpu as pltpu
from jax.sharding import PartitionSpec as P

HEAD_DIM = 128
EXP2_SCALE = HEAD_DIM**-0.5 * math.log2(math.e)
SIDE = 4
BF16 = jnp.bfloat16
F32 = jnp.float32
MIB = 1024 * 1024


def shift_z(array, step):
    pairs = [(y * SIDE + z, y * SIDE + (z + step) % SIDE) for y in range(SIDE) for z in range(SIDE)]
    return lax.ppermute(array, "seq", pairs)


def shift_y(array, step):
    pairs = [(y * SIDE + z, (y + step) % SIDE * SIDE + z) for y in range(SIDE) for z in range(SIDE)]
    return lax.ppermute(array, "seq", pairs)


def whole(shape):
    return pl.BlockSpec(shape, lambda *_: (0,) * len(shape))


def cut_kernel(*refs, head):
    *in_refs, out_ref = refs
    width = in_refs[0].shape[1] // out_ref.shape[0]
    for piece in range(out_ref.shape[0]):
        start = piece * width + head * HEAD_DIM
        for which, ref in enumerate(in_refs):
            out_ref[piece, which] = ref[:, start : start + HEAD_DIM]


def cut(arrays, head):
    tokens, inner = arrays[0].shape
    shape = (SIDE * SIDE, len(arrays), tokens, HEAD_DIM)
    vmem = pl.BlockSpec(memory_space=pltpu.VMEM)
    return pl.pallas_call(
        functools.partial(cut_kernel, head=head),
        in_specs=[vmem] * len(arrays),
        out_specs=vmem,
        out_shape=jax.ShapeDtypeStruct(shape, BF16),
        compiler_params=pltpu.CompilerParams(vmem_limit_bytes=40 * MIB),
        cost_estimate=pl.CostEstimate(
            flops=0, bytes_accessed=4 * len(arrays) * tokens * inner, transcendentals=0
        ),
    )(*arrays)


def join_kernel(*refs):
    in_refs, out_refs = refs[:-2], refs[-2:]
    heads = len(in_refs)
    for head, ref in enumerate(in_refs):
        for piece in range(ref.shape[0]):
            start = (piece * heads + head) * HEAD_DIM
            for which, out_ref in enumerate(out_refs):
                out_ref[:, start : start + HEAD_DIM] = ref[piece, which]


def join(parts):
    count, outputs, tokens, width = parts[0].shape
    shape = jax.ShapeDtypeStruct((tokens, count * len(parts) * width), BF16)
    vmem = pl.BlockSpec(memory_space=pltpu.VMEM)
    return pl.pallas_call(
        join_kernel,
        in_specs=[vmem] * len(parts),
        out_specs=[vmem] * outputs,
        out_shape=[shape] * outputs,
        compiler_params=pltpu.CompilerParams(vmem_limit_bytes=40 * MIB),
        cost_estimate=pl.CostEstimate(
            flops=0, bytes_accessed=4 * count * outputs * tokens * width * len(parts),
            transcendentals=0,
        ),
    )(*parts)


def head_output(queries, keys, wide_values, bias):
    scores = lax.dot_general(
        queries, keys, (((1,), (1,)), ((), ())), preferred_element_type=F32
    )
    if bias is not None:
        scores = scores + bias
    highest = jnp.max(scores, axis=1, keepdims=True)
    weights = jnp.exp2((scores - highest) * EXP2_SCALE).astype(BF16)
    both = jnp.dot(weights, wide_values, preferred_element_type=F32)
    return (both[:, :HEAD_DIM] / both[:, HEAD_DIM:]).astype(BF16)


def attend_kernel(
    query_ref, key_ref, value_ref, cross_ref, text_ref, bias_ref, out_ref, wide_all, *, head, blocks
):
    count = key_ref.shape[0] * key_ref.shape[1]

    @pl.when(pl.program_id(0) == 0)
    def _():
        wide_all[:, :HEAD_DIM] = value_ref[...].reshape(count, HEAD_DIM)
        wide_all[:, HEAD_DIM:] = jnp.ones((count, HEAD_DIM), BF16)

    pieces, _, tokens, _ = out_ref.shape
    width = text_ref.shape[1] // 2
    keys = key_ref[...].reshape(count, HEAD_DIM)
    text_keys = text_ref[:, head * HEAD_DIM : (head + 1) * HEAD_DIM]
    text_values = text_ref[:, width + head * HEAD_DIM : width + (head + 1) * HEAD_DIM]
    wide_text = jnp.concatenate([text_values, jnp.ones_like(text_values)], axis=1)
    step = pieces // blocks
    for block in range(blocks):
        at = slice(block * step, (block + 1) * step)
        queries = query_ref[at].reshape(step * tokens, HEAD_DIM)
        result = head_output(queries, keys, wide_all[...], None)
        out_ref[at, 0] = result.reshape(step, tokens, HEAD_DIM)
        queries = cross_ref[at].reshape(step * tokens, HEAD_DIM)
        result = head_output(queries, text_keys, wide_text, bias_ref[...])
        out_ref[at, 1] = result.reshape(step, tokens, HEAD_DIM)


def attend(by_head, text, bias, head):
    group, _, tokens, _ = by_head.shape
    count = group * tokens
    step = group // 2
    return pl.pallas_call(
        functools.partial(attend_kernel, head=head, blocks=4),
        grid=(group // step,),
        in_specs=[
            pl.BlockSpec((step, None, tokens, HEAD_DIM), lambda i: (i, 0, 0, 0)),
            pl.BlockSpec((group, None, tokens, HEAD_DIM), lambda i: (0, 1, 0, 0)),
            pl.BlockSpec((group, None, tokens, HEAD_DIM), lambda i: (0, 2, 0, 0)),
            pl.BlockSpec((step, None, tokens, HEAD_DIM), lambda i: (i, 3, 0, 0)),
            pl.BlockSpec(text.shape, lambda i: (0, 0)),
            pl.BlockSpec(bias.shape, lambda i: (0, 0)),
        ],
        out_specs=pl.BlockSpec((step, 2, tokens, HEAD_DIM), lambda i: (i, 0, 0, 0)),
        out_shape=jax.ShapeDtypeStruct((group, 2, tokens, HEAD_DIM), BF16),
        scratch_shapes=[pltpu.VMEM((count, 2 * HEAD_DIM), BF16)],
        compiler_params=pltpu.CompilerParams(vmem_limit_bytes=40 * MIB),
        cost_estimate=pl.CostEstimate(
            flops=8 * count * (count + text.shape[0]) * HEAD_DIM,
            bytes_accessed=12 * count * HEAD_DIM,
            transcendentals=count * (count + text.shape[0]),
        ),
    )(by_head, by_head, by_head, by_head, text, bias)


def project_kernel(*refs):
    *text_refs, key_weight_ref, value_weight_ref, out_ref, total = refs
    rows = text_refs[0].shape[0]
    width = key_weight_ref.shape[1]

    @pl.when(pl.program_id(0) == 0)
    def _():
        total[...] = jnp.zeros_like(total)

    for s, ref in enumerate(text_refs):
        for which, weight_ref in enumerate((key_weight_ref, value_weight_ref)):
            total[s * rows : (s + 1) * rows, which * width : (which + 1) * width] += jnp.dot(
                ref[...], weight_ref[...], preferred_element_type=F32
            )

    @pl.when(pl.program_id(0) == pl.num_programs(0) - 1)
    def _():
        out_ref[...] = total[...].astype(BF16)


def project(texts, key_weight, value_weight):
    rows, depth = texts[0].shape
    width = key_weight.shape[1]
    step = 1024
    shape = (len(texts) * rows, 2 * width)
    return pl.pallas_call(
        project_kernel,
        grid=(depth // step,),
        in_specs=[pl.BlockSpec((rows, step), lambda i: (0, i))] * len(texts)
        + [pl.BlockSpec((step, width), lambda i: (i, 0))] * 2,
        out_specs=pl.BlockSpec(shape, lambda i: (0, 0)),
        out_shape=jax.ShapeDtypeStruct(shape, BF16),
        scratch_shapes=[pltpu.VMEM(shape, F32)],
        compiler_params=pltpu.CompilerParams(vmem_limit_bytes=40 * MIB),
        cost_estimate=pl.CostEstimate(
            flops=2 * shape[0] * shape[1] * depth,
            bytes_accessed=2 * depth * (shape[0] + shape[1]),
            transcendentals=0,
        ),
    )(*texts, key_weight, value_weight)


def after(array, *earlier):
    return lax.optimization_barrier((array, *earlier))[0]


def body(
    video_query,
    video_key,
    video_value,
    cross_query,
    text_rows,
    text_block,
    text_length,
    key_weight,
    value_weight,
):
    index = lax.axis_index("seq")
    y, z = index // SIDE, index % SIDE
    text_shard = text_rows.shape[0]
    steps = range(1, SIDE)

    text_from = [shift_z(text_rows, t) for t in steps]
    text_z = jnp.concatenate([text_rows] + text_from, axis=0)
    texts = [text_z] + [shift_y(text_z, s) for s in steps]
    text_own = project(texts, key_weight, value_weight)

    near = jnp.arange(SIDE, dtype=jnp.int32)
    holder = ((y - near) % SIDE * SIDE)[:, None] + ((z - near) % SIDE)[None, :]
    matches = holder[..., None] == jnp.arange(SIDE * SIDE, dtype=jnp.int32)
    blocks = jnp.sum(jnp.where(matches, text_block, 0), axis=-1)
    position = blocks[..., None] * text_shard + jnp.arange(text_shard, dtype=jnp.int32)
    bias = jnp.where(position < text_length[0], 0.0, -jnp.inf).astype(F32).reshape(1, -1)

    arrays = (video_query, video_key, video_value, cross_query)
    swap = functools.partial(
        lax.all_to_all, axis_name="seq", split_axis=0, concat_axis=0, tiled=True
    )
    first = swap(after(cut(arrays, 0), text_z))
    second = swap(after(cut(arrays, 1), first, *texts[1:]))
    first_heads = attend(first, text_own, bias, 0)
    second_heads = attend(after(second, first_heads), text_own, bias, 1)
    self_out, cross_out = join([swap(first_heads), swap(second_heads)])
    return self_out, cross_out


def solution(mesh):
    rows = P(("clip", "seq"), None)
    return jax.shard_map(
        body,
        mesh=mesh,
        in_specs=(
            rows,
            rows,
            rows,
            rows,
            rows,
            P("clip"),
            P("clip"),
            P(None, "seq"),
            P(None, "seq"),
        ),
        out_specs=(rows, rows),
        check_vma=False,
    )
```

```python
import functools
import math

import jax
import jax.numpy as jnp
from jax import lax
from jax.experimental import pallas as pl
from jax.experimental.pallas import tpu as pltpu
from jax.sharding import PartitionSpec as P

HEAD_DIM = 128
EXP2_SCALE = HEAD_DIM**-0.5 * math.log2(math.e)
SIDE = 4
BF16 = jnp.bfloat16
F32 = jnp.float32
MIB = 1024 * 1024


def shift_z(array, step):
    pairs = [(y * SIDE + z, y * SIDE + (z + step) % SIDE) for y in range(SIDE) for z in range(SIDE)]
    return lax.ppermute(array, "seq", pairs)


def shift_y(array, step):
    pairs = [(y * SIDE + z, (y + step) % SIDE * SIDE + z) for y in range(SIDE) for z in range(SIDE)]
    return lax.ppermute(array, "seq", pairs)


def swap_y(array):
    groups = [[y * SIDE + z for y in range(SIDE)] for z in range(SIDE)]
    return lax.all_to_all(
        array, "seq", split_axis=0, concat_axis=0, axis_index_groups=groups, tiled=True
    )


def pack_kernel(place_ref, *refs, sources):
    in_refs, second_ref, first_refs = refs[:sources], refs[sources], refs[sources + 1 :]
    z = place_ref[1]
    width = in_refs[0].shape[1] // (SIDE * SIDE)
    for y in range(SIDE):
        for t in range(SIDE):
            column = (y * SIDE + lax.rem(z + t, SIDE)) * width
            for which, ref in enumerate(in_refs):
                at = pl.ds(pl.multiple_of(column, HEAD_DIM), HEAD_DIM)
                first_refs[t][y, which] = ref[:, at]
                at = pl.ds(pl.multiple_of(column + HEAD_DIM, HEAD_DIM), HEAD_DIM)
                second_ref[y, t, which] = ref[:, at]


def pack(place, arrays):
    tokens, inner = arrays[0].shape
    piece = (len(arrays), tokens, HEAD_DIM)
    shapes = [jax.ShapeDtypeStruct((SIDE, SIDE, *piece), BF16)]
    shapes += [jax.ShapeDtypeStruct((SIDE, *piece), BF16)] * SIDE
    vmem = pl.BlockSpec(memory_space=pltpu.VMEM)
    second, *first = pl.pallas_call(
        functools.partial(pack_kernel, sources=len(arrays)),
        in_specs=[pl.BlockSpec(memory_space=pltpu.SMEM)] + [vmem] * len(arrays),
        out_specs=[vmem] * len(shapes),
        out_shape=shapes,
        compiler_params=pltpu.CompilerParams(vmem_limit_bytes=20 * MIB),
        cost_estimate=pl.CostEstimate(
            flops=0, bytes_accessed=4 * len(arrays) * tokens * inner, transcendentals=0
        ),
    )(place, *arrays)
    return first, second


def join_kernel(place_ref, *refs):
    z = place_ref[1]
    first_ref, second_refs, out_refs = refs[0], refs[1 : SIDE + 1], refs[SIDE + 1 :]
    for y in range(SIDE):
        for t in range(SIDE):
            for head in range(2):
                column = (y * SIDE + lax.rem(z + t, SIDE)) * 2 + head
                at = pl.ds(pl.multiple_of(column * HEAD_DIM, HEAD_DIM), HEAD_DIM)
                for which, out_ref in enumerate(out_refs):
                    if head == 0:
                        out_ref[:, at] = first_ref[y, t, which]
                    else:
                        out_ref[:, at] = second_refs[t][y, which]


def join(place, first, second, shape):
    vmem = pl.BlockSpec(memory_space=pltpu.VMEM)
    return pl.pallas_call(
        join_kernel,
        in_specs=[pl.BlockSpec(memory_space=pltpu.SMEM)] + [vmem] * (SIDE + 1),
        out_specs=[vmem] * 2,
        out_shape=[jax.ShapeDtypeStruct(shape, BF16)] * 2,
        compiler_params=pltpu.CompilerParams(vmem_limit_bytes=20 * MIB),
        cost_estimate=pl.CostEstimate(
            flops=0, bytes_accessed=8 * shape[0] * shape[1], transcendentals=0
        ),
    )(place, first, *second)


def head_output(queries, keys, wide_values, bias):
    scores = lax.dot_general(
        queries, keys, (((1,), (1,)), ((), ())), preferred_element_type=F32
    )
    if bias is not None:
        scores = scores + bias
    highest = jnp.max(scores, axis=1, keepdims=True)
    weights = jnp.exp2((scores - highest) * EXP2_SCALE).astype(BF16)
    both = jnp.dot(weights, wide_values, preferred_element_type=F32)
    return (both[:, :HEAD_DIM] / both[:, HEAD_DIM:]).astype(BF16)


def attend_kernel(*refs, head, blocks):
    *piece_refs, text_ref, bias_ref, out_ref, query_all, key_all, wide_all, cross_all = refs
    _, far_count, _, tokens, _ = out_ref.shape

    @pl.when(pl.program_id(0) == 0)
    def _():
        for far in range(SIDE):
            for near in range(SIDE):
                index = far * SIDE + near
                rows = slice(index * tokens, (index + 1) * tokens)
                ref = piece_refs[0].at[far, near] if len(piece_refs) == 1 else piece_refs[far].at[near]
                query_all[rows] = ref[0]
                key_all[rows] = ref[1]
                wide_all[rows, :HEAD_DIM] = ref[2]
                wide_all[rows, HEAD_DIM:] = jnp.ones((tokens, HEAD_DIM), BF16)
                cross_all[rows] = ref[3]

    width = text_ref.shape[1] // 2
    text_keys = text_ref[:, head * HEAD_DIM : (head + 1) * HEAD_DIM]
    text_values = text_ref[:, width + head * HEAD_DIM : width + (head + 1) * HEAD_DIM]
    wide_text = jnp.concatenate([text_values, jnp.ones_like(text_values)], axis=1)
    rows = far_count * SIDE * tokens // blocks
    start = pl.program_id(0) * (far_count * SIDE * tokens)
    for block in range(blocks):
        at = pl.ds(pl.multiple_of(start + block * rows, rows), rows)
        results = (
            head_output(query_all[at, :], key_all[...], wide_all[...], None),
            head_output(cross_all[at, :], text_keys, wide_text, bias_ref[...]),
        )
        for piece in range(rows // tokens):
            index = block * (rows // tokens) + piece
            for which, result in enumerate(results):
                out_ref[index % SIDE, index // SIDE, which] = result[
                    piece * tokens : (piece + 1) * tokens
                ]


def attend(pieces, specs, text, bias, head):
    tokens = pieces[0].shape[-2]
    count = SIDE * SIDE * tokens
    return pl.pallas_call(
        functools.partial(attend_kernel, head=head, blocks=4),
        grid=(2,),
        in_specs=specs
        + [
            pl.BlockSpec(text.shape, lambda i: (0, 0)),
            pl.BlockSpec(bias.shape, lambda i: (0, 0)),
        ],
        out_specs=pl.BlockSpec(
            (SIDE, SIDE // 2, 2, tokens, HEAD_DIM), lambda i: (0, i, 0, 0, 0)
        ),
        out_shape=jax.ShapeDtypeStruct((SIDE, SIDE, 2, tokens, HEAD_DIM), BF16),
        scratch_shapes=[
            pltpu.VMEM((count, HEAD_DIM), BF16),
            pltpu.VMEM((count, HEAD_DIM), BF16),
            pltpu.VMEM((count, 2 * HEAD_DIM), BF16),
            pltpu.VMEM((count, HEAD_DIM), BF16),
        ],
        compiler_params=pltpu.CompilerParams(vmem_limit_bytes=20 * MIB),
        cost_estimate=pl.CostEstimate(
            flops=8 * count * (count + text.shape[0]) * HEAD_DIM,
            bytes_accessed=12 * count * HEAD_DIM,
            transcendentals=count * (count + text.shape[0]),
        ),
    )(*pieces, text, bias)


def project_kernel(*refs):
    *text_refs, key_weight_ref, value_weight_ref, out_ref, total = refs
    rows = text_refs[0].shape[0]
    width = key_weight_ref.shape[1]

    @pl.when(pl.program_id(0) == 0)
    def _():
        total[...] = jnp.zeros_like(total)

    for s, ref in enumerate(text_refs):
        for which, weight_ref in enumerate((key_weight_ref, value_weight_ref)):
            total[s * rows : (s + 1) * rows, which * width : (which + 1) * width] += jnp.dot(
                ref[...], weight_ref[...], preferred_element_type=F32
            )

    @pl.when(pl.program_id(0) == pl.num_programs(0) - 1)
    def _():
        out_ref[...] = total[...].astype(BF16)


def project(texts, key_weight, value_weight):
    rows, depth = texts[0].shape
    width = key_weight.shape[1]
    step = 1024
    shape = (len(texts) * rows, 2 * width)
    return pl.pallas_call(
        project_kernel,
        grid=(depth // step,),
        in_specs=[pl.BlockSpec((rows, step), lambda i: (0, i))] * len(texts)
        + [pl.BlockSpec((step, width), lambda i: (i, 0))] * 2,
        out_specs=pl.BlockSpec(shape, lambda i: (0, 0)),
        out_shape=jax.ShapeDtypeStruct(shape, BF16),
        scratch_shapes=[pltpu.VMEM(shape, F32)],
        compiler_params=pltpu.CompilerParams(vmem_limit_bytes=20 * MIB),
        cost_estimate=pl.CostEstimate(
            flops=2 * shape[0] * shape[1] * depth,
            bytes_accessed=2 * depth * (shape[0] + shape[1]),
            transcendentals=0,
        ),
    )(*texts, key_weight, value_weight)


def after(array, *earlier):
    return lax.optimization_barrier((array, *earlier))[0]


def body(
    video_query,
    video_key,
    video_value,
    cross_query,
    text_rows,
    text_block,
    text_length,
    key_weight,
    value_weight,
):
    index = lax.axis_index("seq")
    y, z = index // SIDE, index % SIDE
    place = jnp.stack([y, z]).astype(jnp.int32)
    text_shard = text_rows.shape[0]
    side = range(SIDE)
    steps = range(1, SIDE)

    text_from = {t: shift_z(text_rows, t) for t in steps}
    text_z = jnp.concatenate([text_rows] + [text_from[t] for t in steps], axis=0)

    arrays = (video_query, video_key, video_value, cross_query)
    first, second = pack(place, arrays)
    second_y = swap_y(second)
    first_z = {0: first[0]}
    for t in steps:
        first_z[t] = shift_z(after(first[t], text_from[t]), t)

    text_y = {0: text_z, 2: shift_y(text_z, 2), 1: shift_y(text_z, 1), 3: shift_y(text_z, 3)}
    text_own = project([text_y[s] for s in side], key_weight, value_weight)

    second_z = {t: shift_z(after(second_y[:, t], first_z[t]), t) for t in steps}
    first_y = swap_y(after(jnp.stack([first_z[t] for t in side], axis=1), *[text_y[s] for s in steps]))

    near = jnp.arange(SIDE, dtype=jnp.int32)
    holder = ((y - near) % SIDE * SIDE)[:, None] + ((z - near) % SIDE)[None, :]
    matches = holder[..., None] == jnp.arange(SIDE * SIDE, dtype=jnp.int32)
    blocks = jnp.sum(jnp.where(matches, text_block, 0), axis=-1)
    position = blocks[..., None] * text_shard + jnp.arange(text_shard, dtype=jnp.int32)
    bias = jnp.where(position < text_length[0], 0.0, -jnp.inf).astype(F32).reshape(1, -1)

    tokens = video_query.shape[0]
    piece = (len(arrays), tokens, HEAD_DIM)
    first_heads = attend(
        [first_y],
        [pl.BlockSpec((SIDE, SIDE, *piece), lambda i: (0, 0, 0, 0, 0))],
        text_own,
        bias,
        0,
    )
    second_heads = attend(
        [second_y] + [second_z[t] for t in steps],
        [pl.BlockSpec((SIDE, None, *piece), lambda i: (0, 0, 0, 0, 0))]
        + [pl.BlockSpec((SIDE, *piece), lambda i: (0, 0, 0, 0))] * (SIDE - 1),
        text_own,
        bias,
        1,
    )
    first_back = {0: first_heads[0]}
    for t in steps:
        first_back[t] = shift_z(first_heads[t], -t)
    second_back = swap_y(second_heads)
    second_home = {0: second_back[:, 0]}
    for t in steps:
        second_home[t] = shift_z(after(second_back[:, t], first_back[t]), -t)
    first_home = swap_y(
        after(jnp.stack([first_back[t] for t in side], axis=1), second_back)
    )
    self_out, cross_out = join(
        place, first_home, [second_home[t] for t in side], video_query.shape
    )
    return self_out, cross_out


def solution(mesh):
    rows = P(("clip", "seq"), None)
    return jax.shard_map(
        body,
        mesh=mesh,
        in_specs=(
            rows,
            rows,
            rows,
            rows,
            rows,
            P("clip"),
            P("clip"),
            P(None, "seq"),
            P(None, "seq"),
        ),
        out_specs=(rows, rows),
        check_vma=False,
    )
```

```python
import functools
import math

import jax
import jax.numpy as jnp
from jax import lax
from jax.experimental import pallas as pl
from jax.experimental.pallas import tpu as pltpu
from jax.sharding import PartitionSpec as P

HEAD_DIM = 128
EXP2_SCALE = HEAD_DIM**-0.5 * math.log2(math.e)
SIDE = 4
BF16 = jnp.bfloat16
F32 = jnp.float32
MIB = 1024 * 1024


def shift_z(array, step):
    pairs = [(y * SIDE + z, y * SIDE + (z + step) % SIDE) for y in range(SIDE) for z in range(SIDE)]
    return lax.ppermute(array, "seq", pairs)


def shift_y(array, step):
    pairs = [(y * SIDE + z, (y + step) % SIDE * SIDE + z) for y in range(SIDE) for z in range(SIDE)]
    return lax.ppermute(array, "seq", pairs)


def swap_y(array):
    groups = [[y * SIDE + z for y in range(SIDE)] for z in range(SIDE)]
    return lax.all_to_all(
        array, "seq", split_axis=0, concat_axis=0, axis_index_groups=groups, tiled=True
    )


def pack_kernel(place_ref, *refs, sources):
    in_refs, second_ref, first_refs = refs[:sources], refs[sources], refs[sources + 1 :]
    z = place_ref[1]
    width = in_refs[0].shape[1] // (SIDE * SIDE)
    for y in range(SIDE):
        for t in range(SIDE):
            column = (y * SIDE + lax.rem(z + t, SIDE)) * width
            for which, ref in enumerate(in_refs):
                at = pl.ds(pl.multiple_of(column, HEAD_DIM), HEAD_DIM)
                first_refs[t][y, which] = ref[:, at]
                at = pl.ds(pl.multiple_of(column + HEAD_DIM, HEAD_DIM), HEAD_DIM)
                second_ref[y, t, which] = ref[:, at]


def pack(place, arrays):
    tokens, inner = arrays[0].shape
    piece = (len(arrays), tokens, HEAD_DIM)
    shapes = [jax.ShapeDtypeStruct((SIDE, SIDE, *piece), BF16)]
    shapes += [jax.ShapeDtypeStruct((SIDE, *piece), BF16)] * SIDE
    vmem = pl.BlockSpec(memory_space=pltpu.VMEM)
    second, *first = pl.pallas_call(
        functools.partial(pack_kernel, sources=len(arrays)),
        in_specs=[pl.BlockSpec(memory_space=pltpu.SMEM)] + [vmem] * len(arrays),
        out_specs=[vmem] * len(shapes),
        out_shape=shapes,
        compiler_params=pltpu.CompilerParams(vmem_limit_bytes=20 * MIB),
        cost_estimate=pl.CostEstimate(
            flops=0, bytes_accessed=4 * len(arrays) * tokens * inner, transcendentals=0
        ),
    )(place, *arrays)
    return first, second


def join_kernel(place_ref, *refs):
    z = place_ref[1]
    first_ref, second_refs, out_refs = refs[0], refs[1 : SIDE + 1], refs[SIDE + 1 :]
    for y in range(SIDE):
        for t in range(SIDE):
            for head in range(2):
                column = (y * SIDE + lax.rem(z + t, SIDE)) * 2 + head
                at = pl.ds(pl.multiple_of(column * HEAD_DIM, HEAD_DIM), HEAD_DIM)
                for which, out_ref in enumerate(out_refs):
                    if head == 0:
                        out_ref[:, at] = first_ref[y, t, which]
                    else:
                        out_ref[:, at] = second_refs[t][y, which]


def join(place, first, second, shape):
    vmem = pl.BlockSpec(memory_space=pltpu.VMEM)
    return pl.pallas_call(
        join_kernel,
        in_specs=[pl.BlockSpec(memory_space=pltpu.SMEM)] + [vmem] * (SIDE + 1),
        out_specs=[vmem] * 2,
        out_shape=[jax.ShapeDtypeStruct(shape, BF16)] * 2,
        compiler_params=pltpu.CompilerParams(vmem_limit_bytes=20 * MIB),
        cost_estimate=pl.CostEstimate(
            flops=0, bytes_accessed=8 * shape[0] * shape[1], transcendentals=0
        ),
    )(place, first, *second)


def head_output(queries, keys, wide_values, bias):
    scores = lax.dot_general(
        queries, keys, (((1,), (1,)), ((), ())), preferred_element_type=F32
    )
    if bias is not None:
        scores = scores + bias
    highest = jnp.max(scores, axis=1, keepdims=True)
    weights = jnp.exp2((scores - highest) * EXP2_SCALE).astype(BF16)
    both = jnp.dot(weights, wide_values, preferred_element_type=F32)
    return (both[:, :HEAD_DIM] / both[:, HEAD_DIM:]).astype(BF16)


def attend_kernel(*refs, head, blocks):
    *piece_refs, text_ref, bias_ref, out_ref, query_all, key_all, wide_all, cross_all = refs
    _, far_count, _, tokens, _ = out_ref.shape

    @pl.when(pl.program_id(0) == 0)
    def _():
        for far in range(SIDE):
            for near in range(SIDE):
                index = far * SIDE + near
                rows = slice(index * tokens, (index + 1) * tokens)
                ref = piece_refs[0].at[far, near] if len(piece_refs) == 1 else piece_refs[far].at[near]
                query_all[rows] = ref[0]
                key_all[rows] = ref[1]
                wide_all[rows, :HEAD_DIM] = ref[2]
                wide_all[rows, HEAD_DIM:] = jnp.ones((tokens, HEAD_DIM), BF16)
                cross_all[rows] = ref[3]

    width = text_ref.shape[1] // 2
    text_keys = text_ref[:, head * HEAD_DIM : (head + 1) * HEAD_DIM]
    text_values = text_ref[:, width + head * HEAD_DIM : width + (head + 1) * HEAD_DIM]
    wide_text = jnp.concatenate([text_values, jnp.ones_like(text_values)], axis=1)
    rows = far_count * SIDE * tokens // blocks
    start = pl.program_id(0) * (far_count * SIDE * tokens)
    for block in range(blocks):
        at = pl.ds(pl.multiple_of(start + block * rows, rows), rows)
        results = (
            head_output(query_all[at, :], key_all[...], wide_all[...], None),
            head_output(cross_all[at, :], text_keys, wide_text, bias_ref[...]),
        )
        for piece in range(rows // tokens):
            index = block * (rows // tokens) + piece
            for which, result in enumerate(results):
                out_ref[index % SIDE, index // SIDE, which] = result[
                    piece * tokens : (piece + 1) * tokens
                ]


def attend(pieces, specs, text, bias, head):
    tokens = pieces[0].shape[-2]
    count = SIDE * SIDE * tokens
    return pl.pallas_call(
        functools.partial(attend_kernel, head=head, blocks=4),
        grid=(2,),
        in_specs=specs
        + [
            pl.BlockSpec(text.shape, lambda i: (0, 0)),
            pl.BlockSpec(bias.shape, lambda i: (0, 0)),
        ],
        out_specs=pl.BlockSpec(
            (SIDE, SIDE // 2, 2, tokens, HEAD_DIM), lambda i: (0, i, 0, 0, 0)
        ),
        out_shape=jax.ShapeDtypeStruct((SIDE, SIDE, 2, tokens, HEAD_DIM), BF16),
        scratch_shapes=[
            pltpu.VMEM((count, HEAD_DIM), BF16),
            pltpu.VMEM((count, HEAD_DIM), BF16),
            pltpu.VMEM((count, 2 * HEAD_DIM), BF16),
            pltpu.VMEM((count, HEAD_DIM), BF16),
        ],
        compiler_params=pltpu.CompilerParams(vmem_limit_bytes=20 * MIB),
        cost_estimate=pl.CostEstimate(
            flops=8 * count * (count + text.shape[0]) * HEAD_DIM,
            bytes_accessed=12 * count * HEAD_DIM,
            transcendentals=count * (count + text.shape[0]),
        ),
    )(*pieces, text, bias)


def project_kernel(*refs):
    *text_refs, key_weight_ref, value_weight_ref, out_ref, total = refs
    rows = text_refs[0].shape[0]
    width = key_weight_ref.shape[1]

    @pl.when(pl.program_id(0) == 0)
    def _():
        total[...] = jnp.zeros_like(total)

    for s, ref in enumerate(text_refs):
        for which, weight_ref in enumerate((key_weight_ref, value_weight_ref)):
            total[s * rows : (s + 1) * rows, which * width : (which + 1) * width] += jnp.dot(
                ref[...], weight_ref[...], preferred_element_type=F32
            )

    @pl.when(pl.program_id(0) == pl.num_programs(0) - 1)
    def _():
        out_ref[...] = total[...].astype(BF16)


def project(texts, key_weight, value_weight):
    rows, depth = texts[0].shape
    width = key_weight.shape[1]
    step = 1024
    shape = (len(texts) * rows, 2 * width)
    return pl.pallas_call(
        project_kernel,
        grid=(depth // step,),
        in_specs=[pl.BlockSpec((rows, step), lambda i: (0, i))] * len(texts)
        + [pl.BlockSpec((step, width), lambda i: (i, 0))] * 2,
        out_specs=pl.BlockSpec(shape, lambda i: (0, 0)),
        out_shape=jax.ShapeDtypeStruct(shape, BF16),
        scratch_shapes=[pltpu.VMEM(shape, F32)],
        compiler_params=pltpu.CompilerParams(vmem_limit_bytes=20 * MIB),
        cost_estimate=pl.CostEstimate(
            flops=2 * shape[0] * shape[1] * depth,
            bytes_accessed=2 * depth * (shape[0] + shape[1]),
            transcendentals=0,
        ),
    )(*texts, key_weight, value_weight)


def after(array, *earlier):
    return lax.optimization_barrier((array, *earlier))[0]


def body(
    video_query,
    video_key,
    video_value,
    cross_query,
    text_rows,
    text_block,
    text_length,
    key_weight,
    value_weight,
):
    index = lax.axis_index("seq")
    y, z = index // SIDE, index % SIDE
    place = jnp.stack([y, z]).astype(jnp.int32)
    text_shard = text_rows.shape[0]
    side = range(SIDE)
    steps = range(1, SIDE)

    text_from = {t: shift_z(text_rows, t) for t in steps}
    text_z = jnp.concatenate([text_rows] + [text_from[t] for t in steps], axis=0)

    arrays = (video_query, video_key, video_value, cross_query)
    first, second = pack(place, arrays)
    second_y = swap_y(second)
    first_z = {0: first[0]}
    for t in steps:
        first_z[t] = shift_z(after(first[t], text_from[t]), t)

    text_y = {0: text_z, 2: shift_y(text_z, 2), 1: shift_y(text_z, 1), 3: shift_y(text_z, 3)}
    text_own = project([text_y[s] for s in side], key_weight, value_weight)

    second_z = {t: shift_z(second_y[:, t], t) for t in steps}
    first_y = swap_y(after(jnp.stack([first_z[t] for t in side], axis=1), *[text_y[s] for s in steps]))

    near = jnp.arange(SIDE, dtype=jnp.int32)
    holder = ((y - near) % SIDE * SIDE)[:, None] + ((z - near) % SIDE)[None, :]
    matches = holder[..., None] == jnp.arange(SIDE * SIDE, dtype=jnp.int32)
    blocks = jnp.sum(jnp.where(matches, text_block, 0), axis=-1)
    position = blocks[..., None] * text_shard + jnp.arange(text_shard, dtype=jnp.int32)
    bias = jnp.where(position < text_length[0], 0.0, -jnp.inf).astype(F32).reshape(1, -1)

    tokens = video_query.shape[0]
    piece = (len(arrays), tokens, HEAD_DIM)
    first_heads = attend(
        [first_y],
        [pl.BlockSpec((SIDE, SIDE, *piece), lambda i: (0, 0, 0, 0, 0))],
        text_own,
        bias,
        0,
    )
    second_heads = attend(
        [second_y] + [second_z[t] for t in steps],
        [pl.BlockSpec((SIDE, None, *piece), lambda i: (0, 0, 0, 0, 0))]
        + [pl.BlockSpec((SIDE, *piece), lambda i: (0, 0, 0, 0))] * (SIDE - 1),
        after(text_own, first_heads),
        bias,
        1,
    )
    first_back = {0: first_heads[0]}
    for t in steps:
        first_back[t] = shift_z(first_heads[t], -t)
    second_back = swap_y(second_heads)
    second_home = {0: second_back[:, 0]}
    for t in steps:
        second_home[t] = shift_z(second_back[:, t], -t)
    first_home = swap_y(
        after(jnp.stack([first_back[t] for t in side], axis=1), second_back)
    )
    self_out, cross_out = join(
        place, first_home, [second_home[t] for t in side], video_query.shape
    )
    return self_out, cross_out


def solution(mesh):
    rows = P(("clip", "seq"), None)
    return jax.shard_map(
        body,
        mesh=mesh,
        in_specs=(
            rows,
            rows,
            rows,
            rows,
            rows,
            P("clip"),
            P("clip"),
            P(None, "seq"),
            P(None, "seq"),
        ),
        out_specs=(rows, rows),
        check_vma=False,
    )
```

```python
import functools
import math

import jax
import jax.numpy as jnp
from jax import lax
from jax.experimental import pallas as pl
from jax.experimental.pallas import tpu as pltpu
from jax.sharding import PartitionSpec as P

HEAD_DIM = 128
EXP2_SCALE = HEAD_DIM**-0.5 * math.log2(math.e)
SIDE = 4
BF16 = jnp.bfloat16
F32 = jnp.float32
MIB = 1024 * 1024


def shift_z(array, step):
    pairs = [(y * SIDE + z, y * SIDE + (z + step) % SIDE) for y in range(SIDE) for z in range(SIDE)]
    return lax.ppermute(array, "seq", pairs)


def shift_y(array, step):
    pairs = [(y * SIDE + z, (y + step) % SIDE * SIDE + z) for y in range(SIDE) for z in range(SIDE)]
    return lax.ppermute(array, "seq", pairs)


def swap_y(array):
    groups = [[y * SIDE + z for y in range(SIDE)] for z in range(SIDE)]
    return lax.all_to_all(
        array, "seq", split_axis=0, concat_axis=0, axis_index_groups=groups, tiled=True
    )


def pack_kernel(place_ref, *refs, sources):
    in_refs, second_ref, first_refs = refs[:sources], refs[sources], refs[sources + 1 :]
    z = place_ref[1]
    width = in_refs[0].shape[1] // (SIDE * SIDE)
    for y in range(SIDE):
        for t in range(SIDE):
            column = (y * SIDE + lax.rem(z + t, SIDE)) * width
            for which, ref in enumerate(in_refs):
                at = pl.ds(pl.multiple_of(column, HEAD_DIM), HEAD_DIM)
                first_refs[t][y, which] = ref[:, at]
                at = pl.ds(pl.multiple_of(column + HEAD_DIM, HEAD_DIM), HEAD_DIM)
                second_ref[y, t, which] = ref[:, at]


def pack(place, arrays):
    tokens, inner = arrays[0].shape
    piece = (len(arrays), tokens, HEAD_DIM)
    shapes = [jax.ShapeDtypeStruct((SIDE, SIDE, *piece), BF16)]
    shapes += [jax.ShapeDtypeStruct((SIDE, *piece), BF16)] * SIDE
    vmem = pl.BlockSpec(memory_space=pltpu.VMEM)
    second, *first = pl.pallas_call(
        functools.partial(pack_kernel, sources=len(arrays)),
        in_specs=[pl.BlockSpec(memory_space=pltpu.SMEM)] + [vmem] * len(arrays),
        out_specs=[vmem] * len(shapes),
        out_shape=shapes,
        compiler_params=pltpu.CompilerParams(vmem_limit_bytes=20 * MIB),
        cost_estimate=pl.CostEstimate(
            flops=0, bytes_accessed=4 * len(arrays) * tokens * inner, transcendentals=0
        ),
    )(place, *arrays)
    return first, second


def join_kernel(place_ref, *refs):
    z = place_ref[1]
    first_ref, second_refs, out_refs = refs[0], refs[1 : SIDE + 1], refs[SIDE + 1 :]
    for y in range(SIDE):
        for t in range(SIDE):
            for head in range(2):
                column = (y * SIDE + lax.rem(z + t, SIDE)) * 2 + head
                at = pl.ds(pl.multiple_of(column * HEAD_DIM, HEAD_DIM), HEAD_DIM)
                for which, out_ref in enumerate(out_refs):
                    if head == 0:
                        out_ref[:, at] = first_ref[y, t, which]
                    else:
                        out_ref[:, at] = second_refs[t][y, which]


def join(place, first, second, shape):
    vmem = pl.BlockSpec(memory_space=pltpu.VMEM)
    return pl.pallas_call(
        join_kernel,
        in_specs=[pl.BlockSpec(memory_space=pltpu.SMEM)] + [vmem] * (SIDE + 1),
        out_specs=[vmem] * 2,
        out_shape=[jax.ShapeDtypeStruct(shape, BF16)] * 2,
        compiler_params=pltpu.CompilerParams(vmem_limit_bytes=20 * MIB),
        cost_estimate=pl.CostEstimate(
            flops=0, bytes_accessed=8 * shape[0] * shape[1], transcendentals=0
        ),
    )(place, first, *second)


def head_output(queries, keys, wide_values, bias):
    scores = lax.dot_general(
        queries, keys, (((1,), (1,)), ((), ())), preferred_element_type=F32
    )
    if bias is not None:
        scores = scores + bias
    highest = jnp.max(scores, axis=1, keepdims=True)
    weights = jnp.exp2((scores - highest) * EXP2_SCALE).astype(BF16)
    both = jnp.dot(weights, wide_values, preferred_element_type=F32)
    return (both[:, :HEAD_DIM] / both[:, HEAD_DIM:]).astype(BF16)


def attend_kernel(*refs, head, blocks):
    *piece_refs, text_ref, bias_ref, out_ref, query_all, key_all, wide_all, cross_all = refs
    _, far_count, _, tokens, _ = out_ref.shape

    @pl.when(pl.program_id(0) == 0)
    def _():
        for far in range(SIDE):
            for near in range(SIDE):
                index = far * SIDE + near
                rows = slice(index * tokens, (index + 1) * tokens)
                ref = piece_refs[0].at[far, near] if len(piece_refs) == 1 else piece_refs[far].at[near]
                query_all[rows] = ref[0]
                key_all[rows] = ref[1]
                wide_all[rows, :HEAD_DIM] = ref[2]
                wide_all[rows, HEAD_DIM:] = jnp.ones((tokens, HEAD_DIM), BF16)
                cross_all[rows] = ref[3]

    width = text_ref.shape[1] // 2
    text_keys = text_ref[:, head * HEAD_DIM : (head + 1) * HEAD_DIM]
    text_values = text_ref[:, width + head * HEAD_DIM : width + (head + 1) * HEAD_DIM]
    wide_text = jnp.concatenate([text_values, jnp.ones_like(text_values)], axis=1)
    rows = far_count * SIDE * tokens // blocks
    start = pl.program_id(0) * (far_count * SIDE * tokens)
    for block in range(blocks):
        at = pl.ds(pl.multiple_of(start + block * rows, rows), rows)
        results = (
            head_output(query_all[at, :], key_all[...], wide_all[...], None),
            head_output(cross_all[at, :], text_keys, wide_text, bias_ref[...]),
        )
        for piece in range(rows // tokens):
            index = block * (rows // tokens) + piece
            for which, result in enumerate(results):
                out_ref[index % SIDE, index // SIDE, which] = result[
                    piece * tokens : (piece + 1) * tokens
                ]


def attend(pieces, specs, text, bias, head):
    tokens = pieces[0].shape[-2]
    count = SIDE * SIDE * tokens
    return pl.pallas_call(
        functools.partial(attend_kernel, head=head, blocks=4),
        grid=(2,),
        in_specs=specs
        + [
            pl.BlockSpec(text.shape, lambda i: (0, 0)),
            pl.BlockSpec(bias.shape, lambda i: (0, 0)),
        ],
        out_specs=pl.BlockSpec(
            (SIDE, SIDE // 2, 2, tokens, HEAD_DIM), lambda i: (0, i, 0, 0, 0)
        ),
        out_shape=jax.ShapeDtypeStruct((SIDE, SIDE, 2, tokens, HEAD_DIM), BF16),
        scratch_shapes=[
            pltpu.VMEM((count, HEAD_DIM), BF16),
            pltpu.VMEM((count, HEAD_DIM), BF16),
            pltpu.VMEM((count, 2 * HEAD_DIM), BF16),
            pltpu.VMEM((count, HEAD_DIM), BF16),
        ],
        compiler_params=pltpu.CompilerParams(vmem_limit_bytes=20 * MIB),
        cost_estimate=pl.CostEstimate(
            flops=8 * count * (count + text.shape[0]) * HEAD_DIM,
            bytes_accessed=12 * count * HEAD_DIM,
            transcendentals=count * (count + text.shape[0]),
        ),
    )(*pieces, text, bias)


def project_kernel(*refs):
    *text_refs, key_weight_ref, value_weight_ref, out_ref, total = refs
    rows = text_refs[0].shape[0]
    width = key_weight_ref.shape[1]

    @pl.when(pl.program_id(0) == 0)
    def _():
        total[...] = jnp.zeros_like(total)

    for s, ref in enumerate(text_refs):
        for which, weight_ref in enumerate((key_weight_ref, value_weight_ref)):
            total[s * rows : (s + 1) * rows, which * width : (which + 1) * width] += jnp.dot(
                ref[...], weight_ref[...], preferred_element_type=F32
            )

    @pl.when(pl.program_id(0) == pl.num_programs(0) - 1)
    def _():
        out_ref[...] = total[...].astype(BF16)


def project(texts, key_weight, value_weight):
    rows, depth = texts[0].shape
    width = key_weight.shape[1]
    step = 1024
    shape = (len(texts) * rows, 2 * width)
    return pl.pallas_call(
        project_kernel,
        grid=(depth // step,),
        in_specs=[pl.BlockSpec((rows, step), lambda i: (0, i))] * len(texts)
        + [pl.BlockSpec((step, width), lambda i: (i, 0))] * 2,
        out_specs=pl.BlockSpec(shape, lambda i: (0, 0)),
        out_shape=jax.ShapeDtypeStruct(shape, BF16),
        scratch_shapes=[pltpu.VMEM(shape, F32)],
        compiler_params=pltpu.CompilerParams(vmem_limit_bytes=20 * MIB),
        cost_estimate=pl.CostEstimate(
            flops=2 * shape[0] * shape[1] * depth,
            bytes_accessed=2 * depth * (shape[0] + shape[1]),
            transcendentals=0,
        ),
    )(*texts, key_weight, value_weight)


def after(array, *earlier):
    return lax.optimization_barrier((array, *earlier))[0]


def body(
    video_query,
    video_key,
    video_value,
    cross_query,
    text_rows,
    text_block,
    text_length,
    key_weight,
    value_weight,
):
    index = lax.axis_index("seq")
    y, z = index // SIDE, index % SIDE
    place = jnp.stack([y, z]).astype(jnp.int32)
    text_shard = text_rows.shape[0]
    side = range(SIDE)
    steps = range(1, SIDE)

    text_from = {t: shift_z(text_rows, t) for t in steps}
    text_z = jnp.concatenate([text_rows] + [text_from[t] for t in steps], axis=0)

    arrays = (video_query, video_key, video_value, cross_query)
    first, second = pack(place, arrays)
    second_y = swap_y(second)
    first_z = {0: first[0]}
    for t in steps:
        first_z[t] = shift_z(after(first[t], text_from[t]), t)

    text_y = {0: text_z, 1: shift_y(text_z, 1), 3: shift_y(text_z, 3)}
    text_y[2] = shift_y(after(text_z, second_y), 2)
    text_own = project([text_y[s] for s in side], key_weight, value_weight)

    second_z = {t: shift_z(second_y[:, t], t) for t in steps}
    first_y = swap_y(after(jnp.stack([first_z[t] for t in side], axis=1), text_y[1], text_y[3]))

    near = jnp.arange(SIDE, dtype=jnp.int32)
    holder = ((y - near) % SIDE * SIDE)[:, None] + ((z - near) % SIDE)[None, :]
    matches = holder[..., None] == jnp.arange(SIDE * SIDE, dtype=jnp.int32)
    blocks = jnp.sum(jnp.where(matches, text_block, 0), axis=-1)
    position = blocks[..., None] * text_shard + jnp.arange(text_shard, dtype=jnp.int32)
    bias = jnp.where(position < text_length[0], 0.0, -jnp.inf).astype(F32).reshape(1, -1)

    tokens = video_query.shape[0]
    piece = (len(arrays), tokens, HEAD_DIM)
    first_heads = attend(
        [first_y],
        [pl.BlockSpec((SIDE, SIDE, *piece), lambda i: (0, 0, 0, 0, 0))],
        text_own,
        bias,
        0,
    )
    second_heads = attend(
        [second_y] + [second_z[t] for t in steps],
        [pl.BlockSpec((SIDE, None, *piece), lambda i: (0, 0, 0, 0, 0))]
        + [pl.BlockSpec((SIDE, *piece), lambda i: (0, 0, 0, 0))] * (SIDE - 1),
        after(text_own, first_heads),
        bias,
        1,
    )
    first_back = {0: first_heads[0]}
    for t in steps:
        first_back[t] = shift_z(first_heads[t], -t)
    second_back = swap_y(second_heads)
    second_home = {0: second_back[:, 0]}
    for t in steps:
        second_home[t] = shift_z(second_back[:, t], -t)
    first_home = swap_y(
        after(jnp.stack([first_back[t] for t in side], axis=1), second_back)
    )
    self_out, cross_out = join(
        place, first_home, [second_home[t] for t in side], video_query.shape
    )
    return self_out, cross_out


def solution(mesh):
    rows = P(("clip", "seq"), None)
    return jax.shard_map(
        body,
        mesh=mesh,
        in_specs=(
            rows,
            rows,
            rows,
            rows,
            rows,
            P("clip"),
            P("clip"),
            P(None, "seq"),
            P(None, "seq"),
        ),
        out_specs=(rows, rows),
        check_vma=False,
    )
```

```python
import functools
import math

import jax
import jax.numpy as jnp
from jax import lax
from jax.experimental import pallas as pl
from jax.experimental.pallas import tpu as pltpu
from jax.sharding import PartitionSpec as P

HEAD_DIM = 128
EXP2_SCALE = HEAD_DIM**-0.5 * math.log2(math.e)
SIDE = 4
BF16 = jnp.bfloat16
F32 = jnp.float32
MIB = 1024 * 1024


def shift_z(array, step):
    pairs = [(y * SIDE + z, y * SIDE + (z + step) % SIDE) for y in range(SIDE) for z in range(SIDE)]
    return lax.ppermute(array, "seq", pairs)


def shift_y(array, step):
    pairs = [(y * SIDE + z, (y + step) % SIDE * SIDE + z) for y in range(SIDE) for z in range(SIDE)]
    return lax.ppermute(array, "seq", pairs)


def swap_y(array):
    groups = [[y * SIDE + z for y in range(SIDE)] for z in range(SIDE)]
    return lax.all_to_all(
        array, "seq", split_axis=0, concat_axis=0, axis_index_groups=groups, tiled=True
    )


def pack_kernel(place_ref, *refs, sources):
    in_refs, second_ref, first_refs = refs[:sources], refs[sources], refs[sources + 1 :]
    z = place_ref[1]
    width = in_refs[0].shape[1] // (SIDE * SIDE)
    for y in range(SIDE):
        for t in range(SIDE):
            column = (y * SIDE + lax.rem(z + t, SIDE)) * width
            for which, ref in enumerate(in_refs):
                at = pl.ds(pl.multiple_of(column, HEAD_DIM), HEAD_DIM)
                first_refs[t][y, which] = ref[:, at]
                at = pl.ds(pl.multiple_of(column + HEAD_DIM, HEAD_DIM), HEAD_DIM)
                second_ref[y, t, which] = ref[:, at]


def pack(place, arrays):
    tokens, inner = arrays[0].shape
    piece = (len(arrays), tokens, HEAD_DIM)
    shapes = [jax.ShapeDtypeStruct((SIDE, SIDE, *piece), BF16)]
    shapes += [jax.ShapeDtypeStruct((SIDE, *piece), BF16)] * SIDE
    vmem = pl.BlockSpec(memory_space=pltpu.VMEM)
    second, *first = pl.pallas_call(
        functools.partial(pack_kernel, sources=len(arrays)),
        in_specs=[pl.BlockSpec(memory_space=pltpu.SMEM)] + [vmem] * len(arrays),
        out_specs=[vmem] * len(shapes),
        out_shape=shapes,
        compiler_params=pltpu.CompilerParams(vmem_limit_bytes=20 * MIB),
        cost_estimate=pl.CostEstimate(
            flops=0, bytes_accessed=4 * len(arrays) * tokens * inner, transcendentals=0
        ),
    )(place, *arrays)
    return first, second


def join_kernel(place_ref, *refs):
    z = place_ref[1]
    first_ref, second_refs, out_refs = refs[0], refs[1 : SIDE + 1], refs[SIDE + 1 :]
    for y in range(SIDE):
        for t in range(SIDE):
            for head in range(2):
                column = (y * SIDE + lax.rem(z + t, SIDE)) * 2 + head
                at = pl.ds(pl.multiple_of(column * HEAD_DIM, HEAD_DIM), HEAD_DIM)
                for which, out_ref in enumerate(out_refs):
                    if head == 0:
                        out_ref[:, at] = first_ref[y, t, which]
                    else:
                        out_ref[:, at] = second_refs[t][y, which]


def join(place, first, second, shape):
    vmem = pl.BlockSpec(memory_space=pltpu.VMEM)
    return pl.pallas_call(
        join_kernel,
        in_specs=[pl.BlockSpec(memory_space=pltpu.SMEM)] + [vmem] * (SIDE + 1),
        out_specs=[vmem] * 2,
        out_shape=[jax.ShapeDtypeStruct(shape, BF16)] * 2,
        compiler_params=pltpu.CompilerParams(vmem_limit_bytes=20 * MIB),
        cost_estimate=pl.CostEstimate(
            flops=0, bytes_accessed=8 * shape[0] * shape[1], transcendentals=0
        ),
    )(place, first, *second)


def head_output(queries, keys, wide_values, bias):
    scores = lax.dot_general(
        queries, keys, (((1,), (1,)), ((), ())), preferred_element_type=F32
    )
    if bias is not None:
        scores = scores + bias
    highest = jnp.max(scores, axis=1, keepdims=True)
    weights = jnp.exp2((scores - highest) * EXP2_SCALE).astype(BF16)
    both = jnp.dot(weights, wide_values, preferred_element_type=F32)
    return (both[:, :HEAD_DIM] / both[:, HEAD_DIM:]).astype(BF16)


def attend_kernel(*refs, head, blocks):
    *piece_refs, text_ref, bias_ref, out_ref, query_all, key_all, wide_all, cross_all = refs
    _, far_count, _, tokens, _ = out_ref.shape

    @pl.when(pl.program_id(0) == 0)
    def _():
        for far in range(SIDE):
            for near in range(SIDE):
                index = far * SIDE + near
                rows = slice(index * tokens, (index + 1) * tokens)
                ref = piece_refs[0].at[far, near] if len(piece_refs) == 1 else piece_refs[far].at[near]
                query_all[rows] = ref[0]
                key_all[rows] = ref[1]
                wide_all[rows, :HEAD_DIM] = ref[2]
                wide_all[rows, HEAD_DIM:] = jnp.ones((tokens, HEAD_DIM), BF16)
                cross_all[rows] = ref[3]

    width = text_ref.shape[1] // 2
    text_keys = text_ref[:, head * HEAD_DIM : (head + 1) * HEAD_DIM]
    text_values = text_ref[:, width + head * HEAD_DIM : width + (head + 1) * HEAD_DIM]
    wide_text = jnp.concatenate([text_values, jnp.ones_like(text_values)], axis=1)
    rows = far_count * SIDE * tokens // blocks
    start = pl.program_id(0) * (far_count * SIDE * tokens)
    for block in range(blocks):
        at = pl.ds(pl.multiple_of(start + block * rows, rows), rows)
        results = (
            head_output(query_all[at, :], key_all[...], wide_all[...], None),
            head_output(cross_all[at, :], text_keys, wide_text, bias_ref[...]),
        )
        for piece in range(rows // tokens):
            index = block * (rows // tokens) + piece
            for which, result in enumerate(results):
                out_ref[index % SIDE, index // SIDE, which] = result[
                    piece * tokens : (piece + 1) * tokens
                ]


def attend(pieces, specs, text, bias, head):
    tokens = pieces[0].shape[-2]
    count = SIDE * SIDE * tokens
    return pl.pallas_call(
        functools.partial(attend_kernel, head=head, blocks=4),
        grid=(2,),
        in_specs=specs
        + [
            pl.BlockSpec(text.shape, lambda i: (0, 0)),
            pl.BlockSpec(bias.shape, lambda i: (0, 0)),
        ],
        out_specs=pl.BlockSpec(
            (SIDE, SIDE // 2, 2, tokens, HEAD_DIM), lambda i: (0, i, 0, 0, 0)
        ),
        out_shape=jax.ShapeDtypeStruct((SIDE, SIDE, 2, tokens, HEAD_DIM), BF16),
        scratch_shapes=[
            pltpu.VMEM((count, HEAD_DIM), BF16),
            pltpu.VMEM((count, HEAD_DIM), BF16),
            pltpu.VMEM((count, 2 * HEAD_DIM), BF16),
            pltpu.VMEM((count, HEAD_DIM), BF16),
        ],
        compiler_params=pltpu.CompilerParams(vmem_limit_bytes=20 * MIB),
        cost_estimate=pl.CostEstimate(
            flops=8 * count * (count + text.shape[0]) * HEAD_DIM,
            bytes_accessed=12 * count * HEAD_DIM,
            transcendentals=count * (count + text.shape[0]),
        ),
    )(*pieces, text, bias)


def project_kernel(*refs):
    *text_refs, key_weight_ref, value_weight_ref, out_ref, total = refs
    rows = text_refs[0].shape[0]
    width = key_weight_ref.shape[1]

    @pl.when(pl.program_id(0) == 0)
    def _():
        total[...] = jnp.zeros_like(total)

    for s, ref in enumerate(text_refs):
        for which, weight_ref in enumerate((key_weight_ref, value_weight_ref)):
            total[s * rows : (s + 1) * rows, which * width : (which + 1) * width] += jnp.dot(
                ref[...], weight_ref[...], preferred_element_type=F32
            )

    @pl.when(pl.program_id(0) == pl.num_programs(0) - 1)
    def _():
        out_ref[...] = total[...].astype(BF16)


def project(texts, key_weight, value_weight):
    rows, depth = texts[0].shape
    width = key_weight.shape[1]
    step = 1024
    shape = (len(texts) * rows, 2 * width)
    return pl.pallas_call(
        project_kernel,
        grid=(depth // step,),
        in_specs=[pl.BlockSpec((rows, step), lambda i: (0, i))] * len(texts)
        + [pl.BlockSpec((step, width), lambda i: (i, 0))] * 2,
        out_specs=pl.BlockSpec(shape, lambda i: (0, 0)),
        out_shape=jax.ShapeDtypeStruct(shape, BF16),
        scratch_shapes=[pltpu.VMEM(shape, F32)],
        compiler_params=pltpu.CompilerParams(vmem_limit_bytes=20 * MIB),
        cost_estimate=pl.CostEstimate(
            flops=2 * shape[0] * shape[1] * depth,
            bytes_accessed=2 * depth * (shape[0] + shape[1]),
            transcendentals=0,
        ),
    )(*texts, key_weight, value_weight)


def after(array, *earlier):
    return lax.optimization_barrier((array, *earlier))[0]


def body(
    video_query,
    video_key,
    video_value,
    cross_query,
    text_rows,
    text_block,
    text_length,
    key_weight,
    value_weight,
):
    index = lax.axis_index("seq")
    y, z = index // SIDE, index % SIDE
    place = jnp.stack([y, z]).astype(jnp.int32)
    text_shard = text_rows.shape[0]
    side = range(SIDE)
    steps = range(1, SIDE)

    text_from = {t: shift_z(text_rows, t) for t in steps}
    text_z = jnp.concatenate([text_rows] + [text_from[t] for t in steps], axis=0)

    arrays = (video_query, video_key, video_value, cross_query)
    first, second = pack(place, arrays)
    second_y = swap_y(second)
    first_z = {0: first[0]}
    for t in steps:
        first_z[t] = shift_z(after(first[t], text_from[t]), t)

    text_y = {0: text_z, 2: shift_y(text_z, 2), 1: shift_y(text_z, 1), 3: shift_y(text_z, 3)}
    text_own = project([text_y[s] for s in side], key_weight, value_weight)

    cuts = {t: second_y[:, t] for t in steps}
    second_z = {t: shift_z(cuts[t], t) for t in steps}
    together = jnp.stack([first_z[t] for t in side], axis=1)
    first_y = swap_y(after(together, *[text_y[s] for s in steps], *cuts.values()))

    near = jnp.arange(SIDE, dtype=jnp.int32)
    holder = ((y - near) % SIDE * SIDE)[:, None] + ((z - near) % SIDE)[None, :]
    matches = holder[..., None] == jnp.arange(SIDE * SIDE, dtype=jnp.int32)
    blocks = jnp.sum(jnp.where(matches, text_block, 0), axis=-1)
    position = blocks[..., None] * text_shard + jnp.arange(text_shard, dtype=jnp.int32)
    bias = jnp.where(position < text_length[0], 0.0, -jnp.inf).astype(F32).reshape(1, -1)

    tokens = video_query.shape[0]
    piece = (len(arrays), tokens, HEAD_DIM)
    first_heads = attend(
        [first_y],
        [pl.BlockSpec((SIDE, SIDE, *piece), lambda i: (0, 0, 0, 0, 0))],
        text_own,
        bias,
        0,
    )
    second_heads = attend(
        [second_y] + [second_z[t] for t in steps],
        [pl.BlockSpec((SIDE, None, *piece), lambda i: (0, 0, 0, 0, 0))]
        + [pl.BlockSpec((SIDE, *piece), lambda i: (0, 0, 0, 0))] * (SIDE - 1),
        after(text_own, first_heads),
        bias,
        1,
    )
    first_back = {0: first_heads[0]}
    for t in steps:
        first_back[t] = shift_z(first_heads[t], -t)
    second_back = swap_y(second_heads)
    second_home = {0: second_back[:, 0]}
    for t in steps:
        second_home[t] = shift_z(second_back[:, t], -t)
    first_home = swap_y(
        after(jnp.stack([first_back[t] for t in side], axis=1), second_home[1])
    )
    self_out, cross_out = join(
        place, first_home, [second_home[t] for t in side], video_query.shape
    )
    return self_out, cross_out


def solution(mesh):
    rows = P(("clip", "seq"), None)
    return jax.shard_map(
        body,
        mesh=mesh,
        in_specs=(
            rows,
            rows,
            rows,
            rows,
            rows,
            P("clip"),
            P("clip"),
            P(None, "seq"),
            P(None, "seq"),
        ),
        out_specs=(rows, rows),
        check_vma=False,
    )
```
